32 devices in a mesh: groups: 2 (over x), occ: 16 (over z, y, core).
Axes of the slice: x: 2, y: 2, z: 4, core: 2. Of those that a mesh axis runs over, the one named last changes fastest.
Arguments:
- factors: bfloat16 [32, 2, 512, 1024], P(('groups', 'occ')), parts along dimension 0, may hold values from -1.1953125 to 1.1953125
- occ_count: int32 [32], P('groups'), parts along dimension 0, may hold values from 1 to 2, as said below
- e_occ: float32 [32, 2], P('groups'), parts along dimension 0, may hold values from -2 to -0.3
- e_vir: float32 [1024], P('groups'), parts along dimension 0, may hold values from 0.5 to 3
- pair_flags: int32 [32, 2], P('groups'), parts along dimension 0, may hold values 0 or 1
Outputs:
- gamma_three: float32 [32, 2, 512, 1024], P(('groups', 'occ')), parts along dimension 0
- aux_density: float32 [2048, 1024], P(('groups', 'occ')), parts along dimension 0
The draws below stay inside these ranges and needn't reach their ends.
There are 2 independent parts, one for each index of `groups`. The reference program is written for one: setup_inputs(seed, part) draws one part's arguments, and reference() takes and returns one part's arrays. A program takes and returns all parts, laid end to end along the dimension named above; each array names one. Nothing has to cross between parts.
Inputs may be any that keep to these rules, and one draw needn't show every extreme that they name: `occ_count`: some block has 2 live orbitals and some block has 1.
All inputs are finite; a program needn't handle non-finite values.
Results may differ from the reference program's by a relative error of at most 0.002.
Values may be sent and summed in bfloat16 or wider, within the bound.
A program may use at most 128 MiB of HBM per device.

```python
import jax
import jax.numpy as jnp
from jax import lax

VIRTUAL = 512
AUXILIARY = 1024
ORBITALS = 2
PAIR_SPAN = 2
BLOCKS = 16


def draw_occ_count(key, part):
    first, second, third = jax.random.split(jax.random.fold_in(key, 17), 3)
    counts = jax.random.randint(first, (BLOCKS,), 1, ORBITALS + 1)
    full_at = jax.random.randint(second, (), 0, BLOCKS)
    single_at = (full_at + 1 + jax.random.randint(third, (), 0, BLOCKS - 1)) % BLOCKS
    places = jnp.arange(BLOCKS)
    counts = jnp.where(places == full_at, ORBITALS, counts)
    counts = jnp.where(places == single_at, 1, counts)
    return counts.astype(jnp.int32)


def touch_ends(entries, own_key, least, largest):
    index_at = [jax.random.randint(jax.random.fold_in(own_key, axis), (), 0, length) for axis, length in enumerate(entries.shape)]
    widest = entries.shape.index(max(entries.shape))
    neighbour = index_at[:widest] + [(index_at[widest] + 1) % entries.shape[widest]] + index_at[widest + 1:]
    return entries.at[tuple(index_at)].set(least).at[tuple(neighbour)].set(largest)


def shard_levels(key, extent, shards, smallest, high):
    level = 1.0
    for position, blocks in shards:
        steps = jax.random.uniform(jax.random.fold_in(jax.random.fold_in(key, 6), position), (blocks,), jnp.float32, smallest / len(shards), high / len(shards))
        level = level * jnp.repeat(jnp.exp(steps), extent[position] // blocks).reshape((-1,) + (1,) * (len(extent) - 1 - position))
    return level


def bell_draw(stream_key, dims, width, limit, pieces=(), held_as=jnp.bfloat16):
    drawn = width * jax.random.normal(stream_key, dims, jnp.float32)
    if pieces:
        drawn = drawn * shard_levels(stream_key, dims, pieces, -0.22, 0.18)
    return jnp.clip(drawn, -limit, limit).astype(held_as)


def setup_inputs(seed: int = 0, part: int = 0) -> dict:
    streams_of = jax.random.split(jax.random.key(seed), 6)
    part_splits = jax.random.split(jax.random.fold_in(streams_of[5], part), 6)
    factors = bell_draw(part_splits[0], (BLOCKS, ORBITALS, VIRTUAL, AUXILIARY), 0.15, 1.1953125, ((0, 16),))
    occ_count = draw_occ_count(jax.random.fold_in(jax.random.fold_in(streams_of[5], part), 71), part)
    e_occ = jnp.clip(jax.random.uniform(part_splits[2], (BLOCKS, ORBITALS), jnp.float32, -2.0, -0.3), -2.0, -0.3)
    e_vir = jnp.clip(jax.random.uniform(part_splits[3], (VIRTUAL,), jnp.float32, 0.5, 3.0), 0.5, 3.0)
    pair_flags = touch_ends((jax.random.randint(part_splits[4], (BLOCKS, PAIR_SPAN), 0, 2) < 1).astype(jnp.int32), jax.random.fold_in(part_splits[4], 1), 0, 1)
    return dict(factors=factors, occ_count=occ_count, e_occ=e_occ, e_vir=e_vir, pair_flags=pair_flags)


def pair_terms(left_block, right_block, left_energy, right_energy, e_vir, flag):
    left_wide = left_block.astype(jnp.float32)
    right_wide = right_block.astype(jnp.float32)
    integrals = jnp.einsum('ovx,pwx->opvw', left_wide, right_wide)
    virt_sum = e_vir[:, None] + e_vir[None, :]
    denominator = virt_sum[None, None, :, :] - left_energy[:, None, None, None] - right_energy[None, :, None, None]
    amplitudes = -integrals / denominator
    weighted = (flag.astype(jnp.float32) * (2.0 * amplitudes - jnp.swapaxes(amplitudes, 2, 3))).astype(jnp.bfloat16)
    weighted_wide = weighted.astype(jnp.float32)
    update_left = jnp.einsum('opvw,pwx->ovx', weighted_wide, right_wide)
    update_right = jnp.einsum('opvw,ovx->pwx', weighted_wide, left_wide)
    return update_left, update_right


def reference(factors, occ_count, e_occ, e_vir, pair_flags):
    orbital = jnp.arange(ORBITALS, dtype=jnp.int32)
    alive = orbital[None, :] < occ_count[:, None]
    live = jnp.where(alive[:, :, None, None], factors, jnp.zeros_like(factors))
    gamma = jnp.zeros(factors.shape, jnp.float32)
    index = jnp.arange(BLOCKS, dtype=jnp.int32)
    for offset in range(1, PAIR_SPAN + 1):
        def one_pair(block):
            partner = ((block + offset) % BLOCKS).astype(jnp.int32)
            return pair_terms(live[block], live[partner], e_occ[block], e_occ[partner], e_vir, pair_flags[block, offset - 1])

        update_left, update_right = lax.map(one_pair, index)
        gamma = gamma + update_left + jnp.roll(update_right, offset, axis=0)
    rounded = gamma.astype(jnp.bfloat16)
    flat_gamma = rounded.reshape(-1, AUXILIARY)
    flat_live = live.reshape(-1, AUXILIARY)
    product = jnp.dot(flat_gamma.T, flat_live, preferred_element_type=jnp.float32)
    return gamma, product / BLOCKS
```

```python
import jax
import jax.numpy as jnp
from jax import lax
from jax.sharding import PartitionSpec as P


def swap_core(n):
    return [(i, i ^ 1) for i in range(n)]


def swap_near(n):
    return [(i, i ^ 2) for i in range(n)]


def pass_far(n):
    return [(i, (i + 4) % n if (i // 2) % 2 == 0 else (i - 4) % n) for i in range(n)]


def own_update(own, other, scale, energy, other_energy, e_vir):
    integrals = jnp.einsum("ovx,pwx->opvw", own, other, preferred_element_type=jnp.float32)
    virt_sum = e_vir[:, None] + e_vir[None, :]
    denominator = (
        virt_sum[None, None, :, :]
        - energy[:, None, None, None]
        - other_energy[None, :, None, None]
    )
    amplitudes = -integrals / denominator
    weighted = scale[:, :, None, None] * (2.0 * amplitudes - jnp.swapaxes(amplitudes, 2, 3))
    return jnp.einsum(
        "opvw,pwx->ovx", weighted.astype(jnp.bfloat16), other, preferred_element_type=jnp.float32
    )


def per_device(factors, occ_count, e_occ, e_vir, pair_flags):
    n = lax.axis_size("occ")
    me = lax.axis_index("occ")
    core, near, far = me % 2, (me // 2) % 2, me // 4
    own = factors[0]
    orbitals = own.shape[0]

    beside = lax.ppermute(own, "occ", swap_core(n))
    across = lax.ppermute(own, "occ", swap_near(n))
    beyond = lax.ppermute(across, "occ", pass_far(n))
    relay = jnp.where(near == core, across, beyond)
    last = lax.ppermute(relay, "occ", swap_core(n))

    alive = (jnp.arange(orbitals)[None, :] < occ_count[:, None]).astype(jnp.float32)

    def terms(block, step):
        index = (me + step) % n
        first = jnp.where(step > 0, me, index)
        flag = pair_flags[first, jnp.abs(step) - 1]
        scale = flag.astype(jnp.float32) * alive[me][:, None] * alive[index][None, :]
        return lax.cond(
            flag > 0,
            lambda: own_update(own, block, scale, e_occ[me], e_occ[index], e_vir),
            lambda: jnp.zeros(own.shape, jnp.float32),
        )

    gamma = terms(beside, 1 - 2 * core)
    gamma = gamma + terms(across, 2 - 4 * near)
    gamma = gamma + terms(beyond, 4 * near - 2)
    gamma = gamma + terms(last, 2 * core - 1)

    width = gamma.shape[-1]
    flat_gamma = gamma.astype(jnp.bfloat16).reshape(-1, width)
    product = lax.dot_general(
        flat_gamma, own.reshape(-1, width), (((0,), (0,)), ((), ())), preferred_element_type=jnp.float32
    )
    part = product.reshape(n // 4, 2, 2, width // n, width)
    keep = lax.dynamic_index_in_dim(part, core, 2, False)
    give = lax.dynamic_index_in_dim(part, 1 - core, 2, False)
    part = keep + lax.ppermute(give, "occ", swap_core(n))
    keep = lax.dynamic_index_in_dim(part, near, 1, False)
    give = lax.dynamic_index_in_dim(part, 1 - near, 1, False)
    part = keep + lax.ppermute(give, "occ", swap_near(n))
    total = lax.dynamic_index_in_dim(part, far, 0, False)
    for step in range(1, n // 4):
        give = lax.dynamic_index_in_dim(part, (far + step) % (n // 4), 0, False)
        total = total + lax.ppermute(give, "occ", [(i, (i + 4 * step) % n) for i in range(n)])
    return (gamma[None], total / n)


def solution(mesh):
    placed = (
        P(("groups", "occ"), None, None, None),
        P("groups"),
        P("groups", None),
        P("groups"),
        P("groups", None),
    )
    return jax.shard_map(
        per_device,
        mesh=mesh,
        in_specs=placed,
        out_specs=(P(("groups", "occ"), None, None, None), P(("groups", "occ"), None)),
        check_vma=False,
    )
```

```python
import functools

import jax
import jax.numpy as jnp
from jax import lax
from jax.experimental import pallas as pl
from jax.experimental.pallas import tpu as pltpu
from jax.sharding import PartitionSpec as P

MESH = pl.DeviceIdType.MESH
CHUNKS = 8


def kernel(
    n, occ_ref, e_occ_ref, flag_ref, own_hbm, vir_ref, gamma_hbm, aux_ref,
    own, slots, virt_sum, gamma, turned, prod, core_in, near_out, near_in, far_out, far_in,
    load_sem, save_sem, send_sem, recv_sem, core_send, core_recv, near_send, near_recv, far_send, far_recv,
):
    me = lax.axis_index("occ")
    core, near, far = me % 2, (me // 2) % 2, me // 4
    depth = n // 4
    orbitals, virtual, width = gamma.shape
    rows = own.shape[0] // CHUNKS
    part = width // n
    core_peer = me + 1 - 2 * core
    near_peer = me + 2 - 4 * near
    far_peer = (me + 4 - 8 * near + n) % n
    load = pltpu.make_async_copy(own_hbm, own, load_sem)
    load.start()

    def far_at(step):
        return (me + 4 * step) % n

    barrier = pltpu.get_barrier_semaphore()

    def greet(device):
        pl.semaphore_signal(barrier, inc=1, device_id={"occ": device}, device_id_type=MESH)

    greet(core_peer)
    greet(near_peer)

    @pl.loop(1, depth)
    def _(step):
        greet(far_at(step))

    row = jnp.broadcast_to(vir_ref[...], (virtual, virtual))
    virt_sum[...] = row + row.T
    load.wait()
    pl.semaphore_wait(barrier, depth + 1)

    def piece(source, slot, k, device):
        at = pl.ds(pl.multiple_of(k * rows, rows), rows)
        return pltpu.make_async_remote_copy(
            src_ref=source.at[at], dst_ref=slots.at[slot, at],
            send_sem=send_sem.at[slot, k], recv_sem=recv_sem.at[slot, k],
            device_id={"occ": device}, device_id_type=MESH,
        )

    @pl.loop(0, CHUNKS)
    def _(k):
        piece(own, 1, k, near_peer).start()
        piece(own, 0, k, core_peer).start()

    gamma[...] = jnp.zeros_like(gamma)
    relayed = 1 + (near + core) % 2
    per_orbital = CHUNKS // orbitals

    @pl.loop(0, 4 * orbitals)
    def _(t):
        late = t // (2 * orbitals)
        slot = (1 - late) * (t // orbitals) + late * (2 + t % 2)
        other = (1 - late) * (t % orbitals) + late * ((t - 2 * orbitals) // 2 % orbitals)

        @pl.loop(0, per_orbital)
        def _(j):
            k = other * per_orbital + j
            piece(own, slot, k, core_peer).wait_recv()

            @pl.when(slot == 1)
            def _():
                piece(slots.at[1], 2, k, far_peer).start()

            @pl.when(slot == relayed)
            def _():
                piece(slots.at[slot], 3, k, core_peer).start()

        wide = (slot + 1) // 2 % 2
        step = (1 - 2 * (slot // 2)) * ((1 - wide) * (1 - 2 * core) + wide * (2 - 4 * near))
        index = (me + step + n) % n
        first = (me + (1 - (step + 2) // 3) * (step + n)) % n
        live = flag_ref[first, wide].astype(jnp.float32) * jnp.where(other < occ_ref[index], 1.0, 0.0)
        right = slots[slot, pl.ds(pl.multiple_of(other * virtual, virtual), virtual)]
        for o in range(orbitals):
            scale = live * jnp.where(o < occ_ref[me], 1.0, 0.0)
            integrals = lax.dot_general(
                own[o * virtual:(o + 1) * virtual], right, (((1,), (1,)), ((), ())),
                preferred_element_type=jnp.float32,
            )
            denominator = virt_sum[...] - e_occ_ref[me, o] - e_occ_ref[index, other]
            weighted = (integrals.T - 2.0 * integrals) * (scale / denominator)
            gamma[o] += jnp.dot(weighted.astype(jnp.bfloat16), right, preferred_element_type=jnp.float32)

    save = pltpu.make_async_copy(gamma, gamma_hbm, save_sem)
    save.start()
    for o in range(orbitals):
        turned[:, o * virtual:(o + 1) * virtual] = gamma[o].T.astype(jnp.bfloat16)

    def core_copy(j):
        return pltpu.make_async_remote_copy(
            src_ref=prod.at[j, 1 - core], dst_ref=core_in.at[j],
            send_sem=core_send.at[j], recv_sem=core_recv.at[j],
            device_id={"occ": core_peer}, device_id_type=MESH,
        )

    def near_copy(j):
        return pltpu.make_async_remote_copy(
            src_ref=near_out.at[j], dst_ref=near_in.at[j],
            send_sem=near_send.at[j], recv_sem=near_recv.at[j],
            device_id={"occ": near_peer}, device_id_type=MESH,
        )

    def far_copy(j):
        return pltpu.make_async_remote_copy(
            src_ref=far_out.at[j], dst_ref=far_in.at[j],
            send_sem=far_send.at[j], recv_sem=far_recv.at[j],
            device_id={"occ": far_at(j + 1)}, device_id_type=MESH,
        )

    @pl.loop(0, depth)
    def _(j):
        target = (far + j + 1) % depth
        block = jnp.dot(
            turned[pl.ds(pl.multiple_of(target * 4 * part, 4 * part), 4 * part)], own[...],
            preferred_element_type=jnp.float32,
        )
        for c in range(2):
            for y in range(2):
                at = (2 * y + c) * part
                prod[j, c, y] = block[at:at + part]
        core_copy(j).start()

    @pl.loop(0, depth)
    def _(j):
        core_copy(j).wait_recv()
        near_out[j] = prod[j, core, 1 - near] + core_in[j, 1 - near]
        near_copy(j).start()
        far_out[j] = prod[j, core, near] + core_in[j, near]

    @pl.loop(0, depth - 1)
    def _(j):
        near_copy(j).wait_recv()
        far_out[j] += near_in[j]
        far_copy(j).start()

    near_copy(depth - 1).wait_recv()
    aux_ref[...] = far_out[depth - 1] + near_in[depth - 1]

    @pl.loop(0, depth - 1)
    def _(j):
        far_copy(j).wait_recv()
        aux_ref[...] += far_in[j]

    aux_ref[...] = aux_ref[...] * (1.0 / n)

    @pl.loop(0, CHUNKS)
    def _(k):
        piece(own, 0, k, core_peer).wait_send()
        piece(own, 1, k, near_peer).wait_send()
        piece(own, 2, k, far_peer).wait_send()
        piece(own, 3, k, core_peer).wait_send()

    @pl.loop(0, depth)
    def _(j):
        core_copy(j).wait_send()
        near_copy(j).wait_send()

    @pl.loop(0, depth - 1)
    def _(j):
        far_copy(j).wait_send()

    save.wait()


def per_device(factors, occ_count, e_occ, e_vir, pair_flags):
    n = lax.axis_size("occ")
    _, orbitals, virtual, width = factors.shape
    height = orbitals * virtual
    depth, part = n // 4, width // n
    smem = pl.BlockSpec(memory_space=pltpu.SMEM)
    vmem = pl.BlockSpec(memory_space=pltpu.VMEM)
    anywhere = pl.BlockSpec(memory_space=pl.ANY)
    dma = pltpu.SemaphoreType.DMA
    gamma, aux = pl.pallas_call(
        functools.partial(kernel, n),
        out_shape=(
            jax.ShapeDtypeStruct((orbitals, virtual, width), jnp.float32),
            jax.ShapeDtypeStruct((part, width), jnp.float32),
        ),
        in_specs=[smem, smem, smem, anywhere, vmem],
        out_specs=(anywhere, vmem),
        scratch_shapes=[
            pltpu.VMEM((height, width), jnp.bfloat16),
            pltpu.VMEM((4, height, width), jnp.bfloat16),
            pltpu.VMEM((virtual, virtual), jnp.float32),
            pltpu.VMEM((orbitals, virtual, width), jnp.float32),
            pltpu.VMEM((width, height), jnp.bfloat16),
            pltpu.VMEM((depth, 2, 2, part, width), jnp.float32),
            pltpu.VMEM((depth, 2, part, width), jnp.float32),
            pltpu.VMEM((depth, part, width), jnp.float32),
            pltpu.VMEM((depth, part, width), jnp.float32),
            pltpu.VMEM((depth, part, width), jnp.float32),
            pltpu.VMEM((depth, part, width), jnp.float32),
            dma, dma,
            dma((4, CHUNKS)), dma((4, CHUNKS)),
            dma((depth,)), dma((depth,)),
            dma((depth,)), dma((depth,)),
            dma((depth,)), dma((depth,)),
        ],
        compiler_params=pltpu.CompilerParams(
            collective_id=0, has_side_effects=True, vmem_limit_bytes=56 * 1024 * 1024
        ),
    )(occ_count, e_occ, pair_flags, factors.reshape(height, width), e_vir.reshape(1, virtual))
    return (gamma[None], aux)


def solution(mesh):
    placed = (
        P(("groups", "occ"), None, None, None),
        P("groups"),
        P("groups", None),
        P("groups"),
        P("groups", None),
    )
    return jax.shard_map(
        per_device,
        mesh=mesh,
        in_specs=placed,
        out_specs=(P(("groups", "occ"), None, None, None), P(("groups", "occ"), None)),
        check_vma=False,
    )
```

```python
import functools

import jax
import jax.numpy as jnp
from jax import lax
from jax.experimental import pallas as pl
from jax.experimental.pallas import tpu as pltpu
from jax.sharding import PartitionSpec as P

MESH = pl.DeviceIdType.MESH
CHUNKS = 8


def kernel(
    n, occ_hbm, e_occ_hbm, flag_hbm, own_hbm, vir_hbm, gamma_hbm, aux_ref,
    occ_ref, e_occ_ref, flag_ref, vir_ref,
    own, slots, virt_sum, gamma, turned, prod, core_in, near_out, near_in, far_out, far_in,
    small_sem, load_sem, save_sem, send_sem, recv_sem, core_send, core_recv, near_send, near_recv, far_send, far_recv,
):
    me = lax.axis_index("occ")
    core, near, far = me % 2, (me // 2) % 2, me // 4
    depth = n // 4
    orbitals, virtual, width = gamma.shape
    rows = own.shape[0] // CHUNKS
    part = width // n
    core_peer = me + 1 - 2 * core
    near_peer = me + 2 - 4 * near
    far_peer = (me + 4 - 8 * near + n) % n
    load = pltpu.make_async_copy(own_hbm, own, load_sem)
    load.start()
    pairs = ((occ_hbm, occ_ref), (e_occ_hbm, e_occ_ref), (flag_hbm, flag_ref), (vir_hbm, vir_ref))
    small = [pltpu.make_async_copy(a, b, small_sem.at[i]) for i, (a, b) in enumerate(pairs)]
    for copy in small:
        copy.start()

    def far_at(step):
        return (me + 4 * step) % n

    barrier = pltpu.get_barrier_semaphore()

    def greet(device):
        pl.semaphore_signal(barrier, inc=1, device_id={"occ": device}, device_id_type=MESH)

    greet(core_peer)
    greet(near_peer)

    @pl.loop(1, depth)
    def _(step):
        greet(far_at(step))

    pl.semaphore_wait(barrier, depth + 1)

    def piece(source, slot, k, device):
        at = pl.ds(pl.multiple_of(k * rows, rows), rows)
        return pltpu.make_async_remote_copy(
            src_ref=source.at[at], dst_ref=slots.at[slot, at],
            send_sem=send_sem.at[slot, k], recv_sem=recv_sem.at[slot, k],
            device_id={"occ": device}, device_id_type=MESH,
        )

    @pl.loop(0, CHUNKS)
    def _(k):
        piece(own_hbm, 1, k, near_peer).start()

    @pl.loop(0, CHUNKS)
    def _(k):
        piece(own_hbm, 0, k, core_peer).start()

    for copy in small:
        copy.wait()
    row = jnp.broadcast_to(vir_ref[...], (virtual, virtual))
    virt_sum[...] = row + row.T
    load.wait()
    gamma[...] = jnp.zeros_like(gamma)
    relayed = 1 + (near + core) % 2
    per_orbital = CHUNKS // orbitals

    @pl.loop(0, 4 * orbitals)
    def _(t):
        late = t // (2 * orbitals)
        slot = (1 - late) * (t // orbitals) + late * (2 + t % 2)
        other = (1 - late) * (t % orbitals) + late * ((t - 2 * orbitals) // 2 % orbitals)

        @pl.loop(0, per_orbital)
        def _(j):
            k = other * per_orbital + j
            piece(own, slot, k, core_peer).wait_recv()

            @pl.when(slot == 1)
            def _():
                piece(slots.at[1], 2, k, far_peer).start()

            @pl.when(slot == relayed)
            def _():
                piece(slots.at[slot], 3, k, core_peer).start()

        wide = (slot + 1) // 2 % 2
        step = (1 - 2 * (slot // 2)) * ((1 - wide) * (1 - 2 * core) + wide * (2 - 4 * near))
        index = (me + step + n) % n
        first = (me + (1 - (step + 2) // 3) * (step + n)) % n
        live = flag_ref[wide, first].astype(jnp.float32) * jnp.where(other < occ_ref[index], 1.0, 0.0)
        right = slots[slot, pl.ds(pl.multiple_of(other * virtual, virtual), virtual)]
        for o in range(orbitals):
            scale = live * jnp.where(o < occ_ref[me], 1.0, 0.0)
            integrals = lax.dot_general(
                own[o * virtual:(o + 1) * virtual], right, (((1,), (1,)), ((), ())),
                preferred_element_type=jnp.float32,
            )
            denominator = virt_sum[...] - e_occ_ref[o, me] - e_occ_ref[other, index]
            weighted = (integrals.T - 2.0 * integrals) * (scale / denominator)
            gamma[o] += jnp.dot(weighted.astype(jnp.bfloat16), right, preferred_element_type=jnp.float32)

    save = pltpu.make_async_copy(gamma, gamma_hbm, save_sem)
    save.start()
    for o in range(orbitals):
        turned[:, o * virtual:(o + 1) * virtual] = gamma[o].T.astype(jnp.bfloat16)

    def turn(j):
        last = j // (depth - 1)
        return (1 - last) * ((j + depth // 2 - 1) % (depth - 1) + 1)

    def core_copy(j):
        return pltpu.make_async_remote_copy(
            src_ref=prod.at[j, 1 - core], dst_ref=core_in.at[j],
            send_sem=core_send.at[j], recv_sem=core_recv.at[j],
            device_id={"occ": core_peer}, device_id_type=MESH,
        )

    def near_copy(j):
        return pltpu.make_async_remote_copy(
            src_ref=near_out.at[j], dst_ref=near_in.at[j],
            send_sem=near_send.at[j], recv_sem=near_recv.at[j],
            device_id={"occ": near_peer}, device_id_type=MESH,
        )

    def far_copy(j):
        return pltpu.make_async_remote_copy(
            src_ref=far_out.at[j], dst_ref=far_in.at[j],
            send_sem=far_send.at[j], recv_sem=far_recv.at[j],
            device_id={"occ": far_at(turn(j))}, device_id_type=MESH,
        )

    @pl.loop(0, depth)
    def _(j):
        target = (far + turn(j)) % depth
        block = jnp.dot(
            turned[pl.ds(pl.multiple_of(target * 4 * part, 4 * part), 4 * part)], own[...],
            preferred_element_type=jnp.float32,
        )
        for c in range(2):
            for y in range(2):
                at = (2 * y + c) * part
                prod[j, c, y] = block[at:at + part]
        core_copy(j).start()

    @pl.loop(0, depth)
    def _(j):
        core_copy(j).wait_recv()
        near_out[j] = prod[j, core, 1 - near] + core_in[j, 1 - near]
        near_copy(j).start()
        far_out[j] = prod[j, core, near] + core_in[j, near]

    @pl.loop(0, depth - 1)
    def _(j):
        near_copy(j).wait_recv()
        far_out[j] += near_in[j]
        far_copy(j).start()

    near_copy(depth - 1).wait_recv()
    aux_ref[...] = far_out[depth - 1] + near_in[depth - 1]

    @pl.loop(0, depth - 1)
    def _(j):
        far_copy(j).wait_recv()
        aux_ref[...] += far_in[j]

    aux_ref[...] = aux_ref[...] * (1.0 / n)

    @pl.loop(0, CHUNKS)
    def _(k):
        piece(own, 0, k, core_peer).wait_send()
        piece(own, 1, k, near_peer).wait_send()
        piece(own, 2, k, far_peer).wait_send()
        piece(own, 3, k, core_peer).wait_send()

    @pl.loop(0, depth)
    def _(j):
        core_copy(j).wait_send()
        near_copy(j).wait_send()

    @pl.loop(0, depth - 1)
    def _(j):
        far_copy(j).wait_send()

    save.wait()


def per_device(factors, occ_count, e_occ, e_vir, pair_flags):
    n = lax.axis_size("occ")
    _, orbitals, virtual, width = factors.shape
    height = orbitals * virtual
    depth, part = n // 4, width // n
    vmem = pl.BlockSpec(memory_space=pltpu.VMEM)
    anywhere = pl.BlockSpec(memory_space=pl.ANY)
    dma = pltpu.SemaphoreType.DMA
    gamma, aux = pl.pallas_call(
        functools.partial(kernel, n),
        out_shape=(
            jax.ShapeDtypeStruct((orbitals, virtual, width), jnp.float32),
            jax.ShapeDtypeStruct((part, width), jnp.float32),
        ),
        in_specs=[pl.BlockSpec(memory_space=pltpu.HBM)] * 5,
        out_specs=(anywhere, vmem),
        scratch_shapes=[
            pltpu.SMEM(occ_count.shape, jnp.int32),
            pltpu.SMEM(e_occ.shape[::-1], jnp.float32),
            pltpu.SMEM(pair_flags.shape[::-1], jnp.int32),
            pltpu.VMEM((1, virtual), jnp.float32),
            pltpu.VMEM((height, width), jnp.bfloat16),
            pltpu.VMEM((4, height, width), jnp.bfloat16),
            pltpu.VMEM((virtual, virtual), jnp.float32),
            pltpu.VMEM((orbitals, virtual, width), jnp.float32),
            pltpu.VMEM((width, height), jnp.bfloat16),
            pltpu.VMEM((depth, 2, 2, part, width), jnp.float32),
            pltpu.VMEM((depth, 2, part, width), jnp.float32),
            pltpu.VMEM((depth, part, width), jnp.float32),
            pltpu.VMEM((depth, part, width), jnp.float32),
            pltpu.VMEM((depth, part, width), jnp.float32),
            pltpu.VMEM((depth, part, width), jnp.float32),
            dma((4,)), dma, dma,
            dma((4, CHUNKS)), dma((4, CHUNKS)),
            dma((depth,)), dma((depth,)),
            dma((depth,)), dma((depth,)),
            dma((depth,)), dma((depth,)),
        ],
        compiler_params=pltpu.CompilerParams(
            collective_id=0, has_side_effects=True, vmem_limit_bytes=56 * 1024 * 1024
        ),
    )(occ_count, e_occ.T, pair_flags.T, factors.reshape(height, width), e_vir.reshape(1, virtual))
    return (gamma[None], aux)


def solution(mesh):
    placed = (
        P(("groups", "occ"), None, None, None),
        P("groups"),
        P("groups", None),
        P("groups"),
        P("groups", None),
    )
    return jax.shard_map(
        per_device,
        mesh=mesh,
        in_specs=placed,
        out_specs=(P(("groups", "occ"), None, None, None), P(("groups", "occ"), None)),
        check_vma=False,
    )
```

```python
import functools

import jax
import jax.numpy as jnp
from jax import lax
from jax.experimental import pallas as pl
from jax.experimental.pallas import tpu as pltpu
from jax.sharding import PartitionSpec as P

MESH = pl.DeviceIdType.MESH
CHUNKS = 8


def kernel(
    n, occ_hbm, e_occ_hbm, flag_hbm, own_hbm, vir_hbm, gamma_hbm, aux_ref,
    occ_ref, e_occ_ref, flag_ref, vir_ref,
    own, slots, virt_sum, gamma, turned, prod, core_in, near_out, near_in, far_out, far_in,
    small_sem, load_sem, save_sem, send_sem, recv_sem, core_send, core_recv, near_send, near_recv, far_send, far_recv,
):
    me = lax.axis_index("occ")
    core, near, far = me % 2, (me // 2) % 2, me // 4
    depth = n // 4
    orbitals, virtual, width = gamma.shape
    rows = own.shape[0] // CHUNKS
    part = width // n
    core_peer = me + 1 - 2 * core
    near_peer = me + 2 - 4 * near
    far_peer = (me + 4 - 8 * near + n) % n
    load = pltpu.make_async_copy(own_hbm, own, load_sem)
    load.start()
    pairs = ((occ_hbm, occ_ref), (e_occ_hbm, e_occ_ref), (flag_hbm, flag_ref), (vir_hbm, vir_ref))
    small = [pltpu.make_async_copy(a, b, small_sem.at[i]) for i, (a, b) in enumerate(pairs)]
    for copy in small:
        copy.start()

    def far_at(step):
        return (me + 4 * step) % n

    barrier = pltpu.get_barrier_semaphore()

    def greet(device):
        pl.semaphore_signal(barrier, inc=1, device_id={"occ": device}, device_id_type=MESH)

    greet(core_peer)
    greet(near_peer)

    @pl.loop(1, depth)
    def _(step):
        greet(far_at(step))

    pl.semaphore_wait(barrier, depth + 1)

    def piece(source, slot, k, device):
        at = pl.ds(pl.multiple_of(k * rows, rows), rows)
        return pltpu.make_async_remote_copy(
            src_ref=source.at[at], dst_ref=slots.at[slot, at],
            send_sem=send_sem.at[slot, k], recv_sem=recv_sem.at[slot, k],
            device_id={"occ": device}, device_id_type=MESH,
        )

    @pl.loop(0, CHUNKS)
    def _(k):
        piece(own_hbm, 1, k, near_peer).start()

    @pl.loop(0, CHUNKS)
    def _(k):
        piece(own_hbm, 0, k, core_peer).start()

    for copy in small:
        copy.wait()
    row = jnp.broadcast_to(vir_ref[...], (virtual, virtual))
    virt_sum[...] = row + row.T
    load.wait()
    gamma[...] = jnp.zeros_like(gamma)
    relayed = 1 + (near + core) % 2
    per_orbital = CHUNKS // orbitals

    @pl.loop(0, 4 * orbitals)
    def _(t):
        late = t // (2 * orbitals)
        slot = (1 - late) * (t // orbitals) + late * (2 + t % 2)
        other = (1 - late) * (t % orbitals) + late * ((t - 2 * orbitals) // 2 % orbitals)

        @pl.loop(0, per_orbital)
        def _(j):
            k = other * per_orbital + j
            piece(own, slot, k, core_peer).wait_recv()

            @pl.when(slot == 1)
            def _():
                piece(slots.at[1], 2, k, far_peer).start()

            @pl.when(slot == relayed)
            def _():
                piece(slots.at[slot], 3, k, core_peer).start()

        wide = (slot + 1) // 2 % 2
        step = (1 - 2 * (slot // 2)) * ((1 - wide) * (1 - 2 * core) + wide * (2 - 4 * near))
        index = (me + step + n) % n
        first = (me + (1 - (step + 2) // 3) * (step + n)) % n
        live = flag_ref[wide, first].astype(jnp.float32) * jnp.where(other < occ_ref[index], 1.0, 0.0)
        right = slots[slot, pl.ds(pl.multiple_of(other * virtual, virtual), virtual)]
        for o in range(orbitals):
            scale = live * jnp.where(o < occ_ref[me], 1.0, 0.0)
            integrals = lax.dot_general(
                own[o * virtual:(o + 1) * virtual], right, (((1,), (1,)), ((), ())),
                preferred_element_type=jnp.float32,
            )
            denominator = virt_sum[...] - e_occ_ref[o, me] - e_occ_ref[other, index]
            weighted = (integrals.T - 2.0 * integrals) * (scale / denominator)
            gamma[o] += jnp.dot(weighted.astype(jnp.bfloat16), right, preferred_element_type=jnp.float32)

    save = pltpu.make_async_copy(gamma, gamma_hbm, save_sem)
    save.start()
    for o in range(orbitals):
        turned[:, o * virtual:(o + 1) * virtual] = gamma[o].astype(jnp.bfloat16).T

    def turn(j):
        last = j // (depth - 1)
        return (1 - last) * ((j + depth // 2 - 1) % (depth - 1) + 1)

    def core_copy(j):
        return pltpu.make_async_remote_copy(
            src_ref=prod.at[j, 1 - core], dst_ref=core_in.at[j],
            send_sem=core_send.at[j], recv_sem=core_recv.at[j],
            device_id={"occ": core_peer}, device_id_type=MESH,
        )

    def near_copy(j):
        return pltpu.make_async_remote_copy(
            src_ref=near_out.at[j], dst_ref=near_in.at[j],
            send_sem=near_send.at[j], recv_sem=near_recv.at[j],
            device_id={"occ": near_peer}, device_id_type=MESH,
        )

    def far_copy(j):
        return pltpu.make_async_remote_copy(
            src_ref=far_out.at[j], dst_ref=far_in.at[j],
            send_sem=far_send.at[j], recv_sem=far_recv.at[j],
            device_id={"occ": far_at(turn(j))}, device_id_type=MESH,
        )

    @pl.loop(0, depth + 1)
    def _(j):
        @pl.when(j < depth)
        def _():
            target = (far + turn(j)) % depth
            block = jnp.dot(
                turned[pl.ds(pl.multiple_of(target * 4 * part, 4 * part), 4 * part)], own[...],
                preferred_element_type=jnp.float32,
            )
            for c in range(2):
                for y in range(2):
                    at = (2 * y + c) * part
                    prod[j, c, y] = block[at:at + part]
            core_copy(j).start()

        @pl.when(j > 0)
        def _():
            i = j - 1
            core_copy(i).wait_recv()
            near_out[i] = prod[i, core, 1 - near] + core_in[i, 1 - near]
            near_copy(i).start()
            far_out[i] = prod[i, core, near] + core_in[i, near]

    @pl.loop(0, depth - 1)
    def _(j):
        near_copy(j).wait_recv()
        far_out[j] += near_in[j]
        far_copy(j).start()

    near_copy(depth - 1).wait_recv()
    aux_ref[...] = far_out[depth - 1] + near_in[depth - 1]

    @pl.loop(0, depth - 1)
    def _(j):
        far_copy(j).wait_recv()
        aux_ref[...] += far_in[j]

    aux_ref[...] = aux_ref[...] * (1.0 / n)

    @pl.loop(0, CHUNKS)
    def _(k):
        piece(own, 0, k, core_peer).wait_send()
        piece(own, 1, k, near_peer).wait_send()
        piece(own, 2, k, far_peer).wait_send()
        piece(own, 3, k, core_peer).wait_send()

    @pl.loop(0, depth)
    def _(j):
        core_copy(j).wait_send()
        near_copy(j).wait_send()

    @pl.loop(0, depth - 1)
    def _(j):
        far_copy(j).wait_send()

    save.wait()


def per_device(factors, occ_count, e_occ, e_vir, pair_flags):
    n = lax.axis_size("occ")
    _, orbitals, virtual, width = factors.shape
    height = orbitals * virtual
    depth, part = n // 4, width // n
    vmem = pl.BlockSpec(memory_space=pltpu.VMEM)
    anywhere = pl.BlockSpec(memory_space=pl.ANY)
    dma = pltpu.SemaphoreType.DMA
    gamma, aux = pl.pallas_call(
        functools.partial(kernel, n),
        out_shape=(
            jax.ShapeDtypeStruct((orbitals, virtual, width), jnp.float32),
            jax.ShapeDtypeStruct((part, width), jnp.float32),
        ),
        in_specs=[pl.BlockSpec(memory_space=pltpu.HBM)] * 5,
        out_specs=(anywhere, vmem),
        scratch_shapes=[
            pltpu.SMEM(occ_count.shape, jnp.int32),
            pltpu.SMEM(e_occ.shape[::-1], jnp.float32),
            pltpu.SMEM(pair_flags.shape[::-1], jnp.int32),
            pltpu.VMEM((1, virtual), jnp.float32),
            pltpu.VMEM((height, width), jnp.bfloat16),
            pltpu.VMEM((4, height, width), jnp.bfloat16),
            pltpu.VMEM((virtual, virtual), jnp.float32),
            pltpu.VMEM((orbitals, virtual, width), jnp.float32),
            pltpu.VMEM((width, height), jnp.bfloat16),
            pltpu.VMEM((depth, 2, 2, part, width), jnp.float32),
            pltpu.VMEM((depth, 2, part, width), jnp.float32),
            pltpu.VMEM((depth, part, width), jnp.float32),
            pltpu.VMEM((depth, part, width), jnp.float32),
            pltpu.VMEM((depth, part, width), jnp.float32),
            pltpu.VMEM((depth, part, width), jnp.float32),
            dma((4,)), dma, dma,
            dma((4, CHUNKS)), dma((4, CHUNKS)),
            dma((depth,)), dma((depth,)),
            dma((depth,)), dma((depth,)),
            dma((depth,)), dma((depth,)),
        ],
        compiler_params=pltpu.CompilerParams(
            collective_id=0, has_side_effects=True, vmem_limit_bytes=56 * 1024 * 1024
        ),
    )(occ_count, e_occ.T, pair_flags.T, factors.reshape(height, width), e_vir.reshape(1, virtual))
    return (gamma[None], aux)


def solution(mesh):
    placed = (
        P(("groups", "occ"), None, None, None),
        P("groups"),
        P("groups", None),
        P("groups"),
        P("groups", None),
    )
    return jax.shard_map(
        per_device,
        mesh=mesh,
        in_specs=placed,
        out_specs=(P(("groups", "occ"), None, None, None), P(("groups", "occ"), None)),
        check_vma=False,
    )
```
